256 devices in a mesh: ex: 16 (over z, y_lo), layer: 16 (over y_hi, x, core).
Axes of the slice: x: 4, y: 4 (y_hi: 2, y_lo: 2; y = y_hi * 2 + y_lo), z: 8, core: 2. Of those that a mesh axis runs over, the one named last changes fastest.
Arguments:
- grads: bfloat16 [8192, 8192], P('ex', 'layer')
Outputs:
- gram: float32 [8192, 8192], P('layer', 'ex')
All inputs are finite; a program needn't handle non-finite values.
Results may differ from the reference program's by a relative error of at most 0.0021.
Values may be sent and summed in bfloat16 or wider, within the bound.
No kernel may reach another device: no remote copies, remote signals or barrier semaphores. Data moves between devices by JAX's collectives and lax.ppermute only.
A program may use at most 128 MiB of HBM per device.

```python
import jax
import jax.numpy as jnp
from jax import lax

P_SIZE = 256
LAYERS = 32
EXAMPLES = 8192


def draw_grads(key, part):
    key = jax.random.fold_in(key, 7)
    keys = jax.random.split(key, 3)
    width = LAYERS * P_SIZE
    base = jax.random.normal(keys[0], (EXAMPLES, width + 1), jnp.float32)
    base = jnp.clip(base, -5.0, 5.0)
    rows = jnp.exp(jax.random.uniform(keys[1], (EXAMPLES, 1), jnp.float32, 0.0, 2.3))
    mixed = base[:, 1:] + 0.5 * base[:, :-1]
    columns = jnp.exp(jax.random.uniform(keys[2], (1, width), jnp.float32, 0.0, 1.39))
    return (mixed * columns * rows * 0.25).astype(jnp.bfloat16)


def setup_inputs(seed: int = 0) -> dict:
    arg_keys = jax.random.split(jax.random.key(seed), 2)
    grads = draw_grads(jax.random.fold_in(arg_keys[1], 71), 0)
    return dict(grads=grads)


def precondition(block):
    curv = jnp.dot(block.T.astype(jnp.float32), block.astype(jnp.float32), preferred_element_type=jnp.float32) / EXAMPLES
    curv = curv + 0.1 * jnp.eye(block.shape[1], dtype=jnp.float32)
    chol = jnp.linalg.cholesky(curv)
    right = block.T.astype(jnp.float32)
    inner = lax.linalg.triangular_solve(chol, right, left_side=True, lower=True)
    outer = lax.linalg.triangular_solve(chol, inner, left_side=True, lower=True, transpose_a=True)
    return outer.T.astype(jnp.bfloat16)

def reference(grads):
    pieces = []
    for layer_index in range(LAYERS):
        block = grads[:, layer_index * P_SIZE:(layer_index + 1) * P_SIZE]
        pieces.append(precondition(block))
    precond = jnp.concatenate(pieces, axis=1)
    total = lax.dot_general(precond.astype(jnp.float32), grads.astype(jnp.float32), (((1,), (1,)), ((), ())), preferred_element_type=jnp.float32)
    return total / jnp.float32(LAYERS * P_SIZE)
```

```python
import jax
import jax.numpy as jnp
from jax import lax
from jax.experimental import pallas as pl
from jax.experimental.pallas import tpu as pltpu
from jax.sharding import Mesh, PartitionSpec as P

P_SIZE = 256
HALF = 128
PANEL = 8
RIDGE = 0.1
AXES = ("z", "yl", "yh", "x", "core")
SIZES = (8, 2, 2, 4, 2)
HIGHEST = lax.Precision.HIGHEST


def dot32(a, b):
    return jnp.dot(a, b, precision=HIGHEST, preferred_element_type=jnp.float32)


def invert_block(d):
    n = d.shape[0]
    lane = lax.broadcasted_iota(jnp.int32, (1, n), 1)
    sub = lax.broadcasted_iota(jnp.int32, (PANEL, n), 0)
    for k in range(0, n, PANEL):
        cols = [jnp.broadcast_to(d[:, k + i : k + i + 1], (n, n)) for i in range(PANEL)]
        piv = [c[k : k + PANEL, :] for c in cols]
        for j in range(PANEL):
            rp = 1.0 / piv[j][j : j + 1, :]
            pj = piv[j]
            for i in range(PANEL):
                if i == j:
                    piv[i] = jnp.where(sub == j, rp, -pj * rp)
                else:
                    w = piv[i][j : j + 1, :] * rp
                    piv[i] = jnp.where(sub == j, w, piv[i] - pj * w)
        rows = d[k : k + PANEL, :]
        new = piv[0] * rows[0:1, :]
        for i in range(1, PANEL):
            new = new + piv[i] * rows[i : i + 1, :]
        for i in range(PANEL):
            new = jnp.where(lane == k + i, piv[i], new)
        d = jnp.where((lane >= k) & (lane < k + PANEL), 0.0, d)
        for i in range(PANEL):
            d = d - cols[i] * new[i : i + 1, :]
        parts = [x for x in (d[:k], new, d[k + PANEL :]) if x.shape[0]]
        d = jnp.concatenate(parts, axis=0)
    return d


def inverse_kernel(scale, *refs):
    out = refs[-1]
    total = refs[0][...]
    for r in refs[1:-1]:
        total = total + r[...]
    total = total * scale
    r0 = lax.broadcasted_iota(jnp.int32, (HALF, HALF), 0)
    r1 = lax.broadcasted_iota(jnp.int32, (HALF, HALF), 1)
    ridge = jnp.where(r0 == r1, jnp.float32(RIDGE), 0.0)
    a11 = total[:HALF] + ridge
    a12 = total[HALF : 2 * HALF]
    a22 = total[2 * HALF :] + ridge
    inv = invert_block(a11)
    y = dot32(inv, a12)
    z = invert_block(a22 - dot32(a12.T, y))
    w = -dot32(y, z)
    out[:HALF, :HALF] = inv - dot32(w, y.T)
    out[:HALF, HALF:] = w
    out[HALF:, :HALF] = w.T
    out[HALF:, HALF:] = z


def inverse(pieces, scale):
    vmem = pl.BlockSpec(memory_space=pltpu.VMEM)
    return pl.pallas_call(
        lambda *refs: inverse_kernel(scale, *refs),
        out_shape=jax.ShapeDtypeStruct((P_SIZE, P_SIZE), jnp.float32),
        in_specs=[vmem] * len(pieces),
        out_specs=vmem,
        compiler_params=pltpu.CompilerParams(vmem_limit_bytes=32 * 1024 * 1024),
        cost_estimate=pl.CostEstimate(
            flops=2 * 10**9, bytes_accessed=2 * 10**6, transcendentals=0
        ),
        name="inverse",
    )(*pieces)


def gram_kernel(slot_ref, rows_ref, cols_ref, inv_ref, own_ref, other_ref, acc):
    step = pl.program_id(0)
    rows = rows_ref[0]
    rest = inv_ref[0]
    precond = None
    for _ in range(3):
        part = rest.astype(jnp.bfloat16)
        rest = rest - part.astype(jnp.float32)
        term = jnp.dot(rows, part, preferred_element_type=jnp.float32)
        precond = term if precond is None else precond + term
    precond = precond.astype(jnp.bfloat16)
    tile = lax.dot_general(
        precond, cols_ref[0], (((1,), (1,)), ((), ())), preferred_element_type=jnp.float32
    )

    @pl.when(step == 0)
    def _():
        acc[...] = tile

    @pl.when(step > 0)
    def _():
        acc[...] += tile

    @pl.when(step == pl.num_programs(0) - 1)
    def _():
        half = own_ref.shape[1]
        own_ref[...] = acc[:, :half]
        other_ref[...] = acc[:, half:].astype(jnp.bfloat16)


def partial_gram(slots, rows, cols, inv):
    layers, count, width = rows.shape
    wide = cols.shape[1]
    spec = lambda n, pick: pl.BlockSpec((1, n, width), pick)
    return pl.pallas_call(
        gram_kernel,
        grid_spec=pltpu.PrefetchScalarGridSpec(
            num_scalar_prefetch=1,
            grid=(layers,),
            in_specs=[
                spec(count, lambda t, s: (s[t], 0, 0)),
                spec(wide, lambda t, s: (t, 0, 0)),
                spec(width, lambda t, s: (t, 0, 0)),
            ],
            out_specs=[
                pl.BlockSpec((count, wide // 2), lambda t, s: (0, 0)),
                pl.BlockSpec((count, wide // 2), lambda t, s: (0, 0)),
            ],
            scratch_shapes=[pltpu.VMEM((count, wide), jnp.float32)],
        ),
        out_shape=[
            jax.ShapeDtypeStruct((count, wide // 2), jnp.float32),
            jax.ShapeDtypeStruct((count, wide // 2), jnp.bfloat16),
        ],
        compiler_params=pltpu.CompilerParams(vmem_limit_bytes=32 * 1024 * 1024),
        cost_estimate=pl.CostEstimate(
            flops=8 * 10**9, bytes_accessed=18 * 10**6, transcendentals=0
        ),
        name="partial_gram",
    )(slots, rows, cols, inv)


def shift(value, axis, by):
    size = lax.axis_size(axis)
    return lax.ppermute(value, axis, [(i, (i + by) % size) for i in range(size)])


def flat_index(z, yl, yh, x, core):
    return (((z * 2 + yl) * 2 + yh) * 4 + x) * 2 + core


def transpose_perm(same):
    pairs = []
    for z in range(8):
        for y in range(2):
            for k in range(8):
                for b in range(2):
                    src = flat_index(z, y, k // 4, k % 4, b)
                    parity = b if same else 1 - b
                    dst = flat_index((z - k) % 8, parity, z // 4, z % 4, y)
                    pairs.append((src, dst))
    return pairs


def gather_plane(value):
    far = shift(value, "yh", 1)
    pair = jnp.stack([value, far])
    up = shift(pair, "x", 1)
    down = shift(pair, "x", -1)
    two_a = shift(up[:1], "x", 1)
    two_b = shift(down[1:], "x", -1)
    near = [pair, up, down, two_a, two_b]
    return jnp.concatenate(near + [shift(v, "core", 1) for v in near], axis=0)


def gather_ring(value):
    half = value.shape[0] // 2
    up, down = value, value
    out = {0: value}
    for s in range(1, 4):
        up, down = shift(up, "z", 1), shift(down, "z", -1)
        out[s], out[8 - s] = up, down
    out[4] = jnp.concatenate([shift(up[:half], "z", 1), shift(down[half:], "z", -1)])
    return [out[s] for s in range(8)]


def on_device(grads):
    width = P_SIZE
    z, yl, yh, x, core = (lax.axis_index(a) for a in AXES)
    k = yh * 4 + x
    mine = lax.dynamic_slice_in_dim(grads, yl * width, width, 1)
    other = lax.dynamic_slice_in_dim(grads, (1 - yl) * width, width, 1)
    swapped = shift(other, "yl", 1)
    tile = jnp.concatenate([mine, swapped], axis=0)

    curv = lax.dot_general(
        tile, tile, (((0,), (0,)), ((), ())), preferred_element_type=jnp.float32
    )
    packed = jnp.concatenate(
        [curv[:HALF, :HALF], curv[:HALF, HALF:], curv[HALF:, HALF:]], axis=0
    )
    pieces = gather_ring(packed)

    left = lax.dynamic_slice_in_dim(grads, core * width, width, 1)
    right = lax.dynamic_slice_in_dim(grads, (1 - core) * width, width, 1)
    rows_a = lax.ppermute(left, AXES, transpose_perm(True))
    rows_b = lax.ppermute(right, AXES, transpose_perm(False))
    rows = jnp.concatenate(gather_ring(jnp.stack([rows_a, rows_b])))

    cols = gather_plane(tile)

    inv = inverse(pieces, 1.0 / (tile.shape[0] * 8))
    invs = gather_plane(inv)

    slots = []
    for m in range(2):
        for j, i in ((0, 0), (0, 1), (1, 0), (1, 1), (3, 0), (3, 1), (2, 0), (2, 1)):
            layer_k = (yh ^ i) * 4 + (x - j) % 4
            layer_b = core ^ m
            slots.append(((layer_k - k + z) % 8) * 2 + (layer_b ^ yl))
    slots = jnp.stack(slots).astype(jnp.int32)

    own, sent = partial_gram(slots, rows, cols, invs)
    got = shift(sent, "yl", 1)
    scale = 1.0 / jnp.float32(32 * width)
    return (own + got.astype(jnp.float32)) * scale


def solution(mesh):
    fine = Mesh(mesh.devices.reshape(SIZES), AXES)
    return jax.shard_map(
        on_device,
        mesh=fine,
        in_specs=(P(("z", "yl"), ("yh", "x", "core")),),
        out_specs=P(("yh", "x", "core"), ("z", "yl")),
        check_vma=False,
    )
```

```python
import jax
import jax.numpy as jnp
from jax import lax
from jax.experimental import pallas as pl
from jax.experimental.pallas import tpu as pltpu
from jax.sharding import Mesh, PartitionSpec as P

P_SIZE = 256
HALF = 128
PANEL = 8
RIDGE = 0.1
AXES = ("z", "yl", "yh", "x", "core")
SIZES = (8, 2, 2, 4, 2)
HIGHEST = lax.Precision.HIGHEST


def dot32(a, b):
    return jnp.dot(a, b, precision=HIGHEST, preferred_element_type=jnp.float32)


def invert_block(d):
    n = d.shape[0]
    lane = lax.broadcasted_iota(jnp.int32, (1, n), 1)
    sub = lax.broadcasted_iota(jnp.int32, (PANEL, n), 0)
    for k in range(0, n, PANEL):
        cols = [jnp.broadcast_to(d[:, k + i : k + i + 1], (n, n)) for i in range(PANEL)]
        piv = [c[k : k + PANEL, :] for c in cols]
        for j in range(PANEL):
            rp = 1.0 / piv[j][j : j + 1, :]
            pj = piv[j]
            for i in range(PANEL):
                if i == j:
                    piv[i] = jnp.where(sub == j, rp, -pj * rp)
                else:
                    w = piv[i][j : j + 1, :] * rp
                    piv[i] = jnp.where(sub == j, w, piv[i] - pj * w)
        rows = d[k : k + PANEL, :]
        new = piv[0] * rows[0:1, :]
        for i in range(1, PANEL):
            new = new + piv[i] * rows[i : i + 1, :]
        for i in range(PANEL):
            new = jnp.where(lane == k + i, piv[i], new)
        d = jnp.where((lane >= k) & (lane < k + PANEL), 0.0, d)
        for i in range(PANEL):
            d = d - cols[i] * new[i : i + 1, :]
        parts = [x for x in (d[:k], new, d[k + PANEL :]) if x.shape[0]]
        d = jnp.concatenate(parts, axis=0)
    return d


def inverse_kernel(scale, *refs):
    out = refs[-1]
    whole = [r[...] for r in refs[:-1] if r.shape[0] == out.shape[0]]
    total = jnp.concatenate([r[...] for r in refs[:-1] if r.shape[0] < out.shape[0]], axis=0)
    for w in whole:
        total = total + w
    total = total * scale
    r0 = lax.broadcasted_iota(jnp.int32, (HALF, HALF), 0)
    r1 = lax.broadcasted_iota(jnp.int32, (HALF, HALF), 1)
    ridge = jnp.where(r0 == r1, jnp.float32(RIDGE), 0.0)
    a11 = total[:HALF] + ridge
    a12 = total[HALF : 2 * HALF]
    a22 = total[2 * HALF :] + ridge
    inv = invert_block(a11)
    y = dot32(inv, a12)
    z = invert_block(a22 - dot32(a12.T, y))
    w = -dot32(y, z)
    out[:HALF] = inv - dot32(w, y.T)
    out[HALF : 2 * HALF] = w
    out[2 * HALF :] = z


def inverse(pieces, scale):
    vmem = pl.BlockSpec(memory_space=pltpu.VMEM)
    return pl.pallas_call(
        lambda *refs: inverse_kernel(scale, *refs),
        out_shape=jax.ShapeDtypeStruct((3 * HALF, HALF), jnp.float32),
        in_specs=[vmem] * len(pieces),
        out_specs=vmem,
        compiler_params=pltpu.CompilerParams(vmem_limit_bytes=32 * 1024 * 1024),
        cost_estimate=pl.CostEstimate(
            flops=2 * 10**9, bytes_accessed=2 * 10**6, transcendentals=0
        ),
        name="inverse",
    )(*pieces)


VMEM = pl.BlockSpec(memory_space=pltpu.VMEM)
SMEM = pl.BlockSpec(memory_space=pltpu.SMEM)


def call(kernel, name, shape, flops, *operands, specs=None, aliases=None):
    return pl.pallas_call(
        kernel,
        in_specs=specs or [VMEM] * len(operands),
        out_specs=jax.tree.map(lambda _: VMEM, shape),
        out_shape=shape,
        input_output_aliases=aliases or {},
        compiler_params=pltpu.CompilerParams(vmem_limit_bytes=16 * 1024 * 1024),
        cost_estimate=pl.CostEstimate(
            flops=flops, bytes_accessed=4 * 10**6, transcendentals=0
        ),
        name=name,
    )(*operands)


def split_kernel(*refs):
    out = refs[-1]
    matrices = [r[j] for r in refs[:-1] for j in range(r.shape[0])]
    for t, packed in enumerate(matrices):
        top, off, low = (packed[i * HALF : (i + 1) * HALF] for i in range(3))
        full = jnp.concatenate(
            [jnp.concatenate([top, off], axis=1), jnp.concatenate([off.T, low], axis=1)],
            axis=0,
        )
        for i in range(3):
            part = full.astype(jnp.bfloat16)
            full = full - part.astype(jnp.float32)
            out[t, i * P_SIZE : (i + 1) * P_SIZE] = part


def split(inv):
    layers = sum(i.shape[0] for i in inv)
    shape = jax.ShapeDtypeStruct((layers, 3 * P_SIZE, P_SIZE), jnp.bfloat16)
    return call(split_kernel, "split", shape, 10**6, *inv)


def precond_kernel(first, plan, parts, *refs):
    out = refs[-1]
    rows = [(r, j) for r in refs[:-1] if r.shape[-1] == P_SIZE for j in range(r.shape[0])]
    for slot, (r, j) in enumerate(rows):
        layer, half = plan[0, first + slot], plan[1, first + slot]
        x = r[j]
        total = jnp.dot(
            jnp.concatenate([x, x, x], axis=1), parts[layer], preferred_element_type=jnp.float32
        )
        count = x.shape[0]
        down = pl.ds(pl.multiple_of(half * count, count), count)
        across = pl.ds(pl.multiple_of(layer * P_SIZE, P_SIZE), P_SIZE)
        out[down, across] = total.astype(jnp.bfloat16)


def precondition(plan, first, parts, rows, into=None):
    count = rows[0].shape[1]
    shape = jax.ShapeDtypeStruct((2 * count, parts.shape[0] * P_SIZE), jnp.bfloat16)
    operands = [plan, parts, *rows] + ([] if into is None else [into])
    return call(
        lambda *refs: precond_kernel(first, *refs),
        "precondition",
        shape,
        10**9,
        *operands,
        specs=[SMEM] + [VMEM] * (len(operands) - 1),
        aliases=None if into is None else {len(operands) - 1: 0},
    )


def gram_kernel(start, precond, *refs):
    theirs, mine = refs[-2:]
    half = mine.shape[1]
    cols = [r[j, start : start + half] for r in refs[:-2] for j in range(r.shape[0])]
    total = lax.dot_general(
        precond[...],
        jnp.concatenate(cols, axis=1),
        (((1,), (1,)), ((), ())),
        preferred_element_type=jnp.float32,
    )
    theirs[...] = total[: theirs.shape[0]]
    mine[...] = total[theirs.shape[0] :]


def partial_gram(precond, cols, start):
    half = cols[0].shape[1] // 2
    shape = [jax.ShapeDtypeStruct((precond.shape[0] // 2, half), jnp.float32)] * 2
    return call(
        lambda *refs: gram_kernel(start, *refs), "gram", shape, 2 * 10**9, precond, *cols
    )


def shift(value, axis, by):
    size = lax.axis_size(axis)
    return lax.ppermute(value, axis, [(i, (i + by) % size) for i in range(size)])


def flat_index(z, yl, yh, x, core):
    return (((z * 2 + yl) * 2 + yh) * 4 + x) * 2 + core


def after(values, token):
    return lax.optimization_barrier((values, token))[0]


def transpose_perm(same):
    pairs = []
    for z in range(8):
        for y in range(2):
            for k in range(8):
                for b in range(2):
                    src = flat_index(z, y, k // 4, k % 4, b)
                    p = y if same else 1 - y
                    to = (z + k + 2 * (2 * same + p + b)) % 8
                    pairs.append((src, flat_index(to, p, z // 4, z % 4, b)))
    return pairs


def ring_step(state, last):
    up, down = state
    if last:
        half = up.shape[0] // 2
        return shift(up[:half], "z", 1), shift(down[half:], "z", -1)
    return shift(up, "z", 1), shift(down, "z", -1)


def ring_pieces(steps):
    first, *near, last = steps
    return [first[0]] + [u for u, _ in near] + list(last) + [d for _, d in near[::-1]]


def on_device(grads):
    width = P_SIZE
    z, yl, yh, x, core = (lax.axis_index(a) for a in AXES)
    k = yh * 4 + x
    mine = lax.dynamic_slice_in_dim(grads, yl * width, width, 1)
    other = lax.dynamic_slice_in_dim(grads, (1 - yl) * width, width, 1)
    swapped = shift(other, "yl", 1)
    rows_a = lax.ppermute(mine, AXES, transpose_perm(1))
    rows_b = lax.ppermute(other, AXES, transpose_perm(0))

    far_mine, far_swapped = shift(mine, "yh", 1), shift(swapped, "yh", 1)
    tile = jnp.concatenate([mine, swapped], axis=0)
    pair = jnp.stack([tile, jnp.concatenate([far_mine, far_swapped], axis=0)])
    curv = lax.dot_general(
        tile, tile, (((0,), (0,)), ((), ())), preferred_element_type=jnp.float32
    )
    packed = jnp.concatenate(
        [curv[:HALF, :HALF], curv[:HALF, HALF:], curv[HALF:, HALF:]], axis=0
    )
    curvs = [(packed, packed)]
    curvs.append(after(ring_step(curvs[-1], False), (rows_a, rows_b, pair)))
    curvs.append(ring_step(curvs[-1], False))
    pair = after(pair, curvs[1])
    up, down = shift(pair, "x", 1), shift(pair, "x", -1)
    curvs.append(ring_step(curvs[-1], False))
    curvs.append(ring_step(curvs[-1], True))
    first = after(jnp.stack([rows_a, rows_b]), curvs[4])
    rows = [(first, first)]
    rows.append(ring_step(rows[-1], False))
    inv = inverse(ring_pieces(curvs), 1.0 / (tile.shape[0] * 8))

    inv_far = shift(inv, "yh", 1)
    rows.append(ring_step(after(rows[-1], inv), False))
    cols_two = shift(after(up[:1], inv), "x", 1), shift(after(down[1:], inv), "x", -1)
    inv_pair = after(jnp.stack([inv, inv_far]), cols_two)
    inv_up, inv_down = shift(inv_pair, "x", 1), shift(inv_pair, "x", -1)
    rows.append(ring_step(after(rows[-1], inv_pair), False))
    inv_two = shift(inv_up[:1], "x", 1), shift(inv_down[1:], "x", -1)
    rows.append(ring_step(rows[-1], True))

    rows = ring_pieces(rows)
    near, far_rows = rows[:4] + rows[6:], rows[4:6]
    step = jnp.asarray([0, 0, 1, 1, 2, 2, 3, 3, 5, 5, 6, 6, 7, 7, 4, 4], jnp.int32)[None]
    same = jnp.asarray([1, 0] * 8, jnp.int32)[None]
    layer_k = (z - step - k - 2 * (2 * same + yl + core)) % 8
    d = (x - layer_k) % 4
    place = jnp.where(d < 2, 2 * d, 10 - 2 * d) + ((layer_k // 4) ^ yh)
    mine_half = (core ^ yl ^ same).astype(jnp.int32)
    which = lax.broadcasted_iota(jnp.int32, (2, 16), 0)
    plan = jnp.where(which == 0, place, mine_half)

    cols = [pair, up, down, *cols_two]
    parts = split([inv_pair, inv_up, inv_down, *inv_two])
    precond = precondition(plan, 0, parts, near)
    precond = precondition(plan, 14, parts, far_rows, precond)
    half = mine.shape[0]
    theirs_other, mine_other = partial_gram(precond, cols, half)
    mine_other = mine_other + shift(theirs_other, "core", 1)
    got = shift(mine_other.astype(jnp.bfloat16), "yl", 1)
    theirs_own, mine_own = partial_gram(after(precond, theirs_other), cols, 0)
    mine_own = mine_own + shift(theirs_own, "core", 1)
    scale = 1.0 / jnp.float32(32 * width)
    return (mine_own + got.astype(jnp.float32)) * scale


def solution(mesh):
    fine = Mesh(mesh.devices.reshape(SIZES), AXES)
    return jax.shard_map(
        on_device,
        mesh=fine,
        in_specs=(P(("z", "yl"), ("yh", "x", "core")),),
        out_specs=P(("yh", "x", "core"), ("z", "yl")),
        check_vma=False,
    )
```

```python
import jax
import jax.numpy as jnp
from jax import lax
from jax.experimental import pallas as pl
from jax.experimental.pallas import tpu as pltpu
from jax.sharding import Mesh, PartitionSpec as P

P_SIZE = 256
HALF = 128
QUARTER = 64
PACKED = 320
PANEL = 8
RIDGE = 0.1
AXES = ("z", "yl", "yh", "x", "core")
SIZES = (8, 2, 2, 4, 2)
HIGHEST = lax.Precision.HIGHEST


def dot32(a, b):
    return jnp.dot(a, b, precision=HIGHEST, preferred_element_type=jnp.float32)


def invert_block(d):
    n = d.shape[0]
    lane = lax.broadcasted_iota(jnp.int32, (1, n), 1)
    sub = lax.broadcasted_iota(jnp.int32, (PANEL, n), 0)
    for k in range(0, n, PANEL):
        cols = [jnp.broadcast_to(d[:, k + i : k + i + 1], (n, n)) for i in range(PANEL)]
        piv = [c[k : k + PANEL, :] for c in cols]
        for j in range(PANEL):
            rp = 1.0 / piv[j][j : j + 1, :]
            pj = piv[j]
            for i in range(PANEL):
                if i == j:
                    piv[i] = jnp.where(sub == j, rp, -pj * rp)
                else:
                    w = piv[i][j : j + 1, :] * rp
                    piv[i] = jnp.where(sub == j, w, piv[i] - pj * w)
        rows = d[k : k + PANEL, :]
        new = piv[0] * rows[0:1, :]
        for i in range(1, PANEL):
            new = new + piv[i] * rows[i : i + 1, :]
        for i in range(PANEL):
            new = jnp.where(lane == k + i, piv[i], new)
        d = jnp.where((lane >= k) & (lane < k + PANEL), 0.0, d)
        for i in range(PANEL):
            d = d - cols[i] * new[i : i + 1, :]
        parts = [x for x in (d[:k], new, d[k + PANEL :]) if x.shape[0]]
        d = jnp.concatenate(parts, axis=0)
    return d


def pack(a11, a12, a22):
    q = QUARTER
    corners = jnp.concatenate([a11[q:, q:], a22[q:, q:]], axis=1)
    return jnp.concatenate([a11[:q], a12, a22[:q], corners], axis=0)


def unpack(packed):
    q = QUARTER
    corners = packed[4 * q :]

    def whole(top, corner):
        low = jnp.concatenate([top[:, q:].T, corner], axis=1)
        return jnp.concatenate([top, low], axis=0)

    a11 = whole(packed[:q], corners[:, :q])
    a22 = whole(packed[3 * q : 4 * q], corners[:, q:])
    return a11, packed[q : 3 * q], a22


def ridge():
    r0 = lax.broadcasted_iota(jnp.int32, (HALF, HALF), 0)
    r1 = lax.broadcasted_iota(jnp.int32, (HALF, HALF), 1)
    return jnp.where(r0 == r1, jnp.float32(RIDGE), 0.0)


def inverse_kernel(scale, total, out):
    a11, a12, a22 = unpack(total[...] * scale)
    inv = invert_block(a11 + ridge())
    y = dot32(inv, a12)
    z = invert_block(a22 + ridge() - dot32(a12.T, y))
    w = -dot32(y, z)
    out[...] = pack(inv - dot32(w, y.T), w, z)


VMEM = pl.BlockSpec(memory_space=pltpu.VMEM)
SMEM = pl.BlockSpec(memory_space=pltpu.SMEM)


def call(kernel, name, shape, flops, *operands, specs=None, aliases=None):
    return pl.pallas_call(
        kernel,
        in_specs=specs or [VMEM] * len(operands),
        out_specs=jax.tree.map(lambda _: VMEM, shape),
        out_shape=shape,
        input_output_aliases=aliases or {},
        compiler_params=pltpu.CompilerParams(vmem_limit_bytes=16 * 1024 * 1024),
        cost_estimate=pl.CostEstimate(
            flops=flops, bytes_accessed=4 * 10**6, transcendentals=0
        ),
        name=name,
    )(*operands)


def split_kernel(*refs):
    out = refs[-1]
    matrices = [r[j] for r in refs[:-1] for j in range(r.shape[0])]
    for t, packed in enumerate(matrices):
        top, off, low = unpack(packed)
        full = jnp.concatenate(
            [jnp.concatenate([top, off], axis=1), jnp.concatenate([off.T, low], axis=1)],
            axis=0,
        )
        for i in range(3):
            part = full.astype(jnp.bfloat16)
            full = full - part.astype(jnp.float32)
            out[t, i * P_SIZE : (i + 1) * P_SIZE] = part


def split(inv):
    layers = sum(i.shape[0] for i in inv)
    shape = jax.ShapeDtypeStruct((layers, 3 * P_SIZE, P_SIZE), jnp.bfloat16)
    return call(split_kernel, "split", shape, 10**6, *inv)


def precond_kernel(late, plan, *refs):
    *parts, out = refs[: 2 if late else 1] + (refs[-1],)
    tiles = refs[len(parts) : len(parts) + 8 if late else len(parts) + 7]
    near = parts[0].shape[0]
    slot = 0
    for n, r in enumerate(tiles):
        for j in range(r.shape[0]):
            step = (0, 1, 2, 3, 5, 6, 7, 4)[n]
            layer = plan[j, step]

            def put(part):
                x = r[j]
                total = jnp.dot(
                    jnp.concatenate([x, x, x], axis=1), part, preferred_element_type=jnp.float32
                )
                across = pl.ds(pl.multiple_of(layer * P_SIZE, P_SIZE), P_SIZE)
                count = x.shape[0]
                out[j * count : (j + 1) * count, across] = total.astype(jnp.bfloat16)

            if not late or step == 4:

                @pl.when(layer < near)
                def _():
                    put(parts[0][layer])

            if late:

                @pl.when(layer >= near)
                def _():
                    put(parts[1][layer - near])


def precondition(plan, parts, rows, into=None):
    late = into is not None
    count = rows[0].shape[1]
    shape = jax.ShapeDtypeStruct((2 * count, 8 * P_SIZE), jnp.bfloat16)
    operands = [plan, *parts, *rows] + ([into] if late else [])
    return call(
        lambda *refs: precond_kernel(late, *refs),
        "precondition",
        shape,
        2 * 10**9,
        *operands,
        specs=[SMEM] + [VMEM] * (len(operands) - 1),
        aliases={len(operands) - 1: 0} if late else None,
    )


def gram_kernel(start, precond, *refs):
    theirs, mine = refs[-2:]
    half = mine.shape[1]
    cols = [r[j, start : start + half] for r in refs[:-2] for j in range(r.shape[0])]
    total = lax.dot_general(
        precond[...],
        jnp.concatenate(cols, axis=1),
        (((1,), (1,)), ((), ())),
        preferred_element_type=jnp.float32,
    )
    theirs[...] = total[: theirs.shape[0]]
    mine[...] = total[theirs.shape[0] :]


def partial_gram(precond, cols, start):
    half = cols[0].shape[1] // 2
    shape = [jax.ShapeDtypeStruct((precond.shape[0] // 2, half), jnp.float32)] * 2
    return call(
        lambda *refs: gram_kernel(start, *refs), "gram", shape, 2 * 10**9, precond, *cols
    )


def shift(value, axis, by):
    size = lax.axis_size(axis)
    return lax.ppermute(value, axis, [(i, (i + by) % size) for i in range(size)])


def flat_index(z, yl, yh, x, core):
    return (((z * 2 + yl) * 2 + yh) * 4 + x) * 2 + core


def after(values, token):
    return lax.optimization_barrier((values, token))[0]


def transpose_perm(same):
    pairs = []
    for z in range(8):
        for y in range(2):
            for k in range(8):
                for b in range(2):
                    src = flat_index(z, y, k // 4, k % 4, b)
                    p = y if same else 1 - y
                    to = (z + k + 2 * (2 * same + p + b)) % 8
                    pairs.append((src, flat_index(to, p, z // 4, z % 4, b)))
    return pairs


def shift_apart(up, down, axis, by=1):
    size = lax.axis_size(axis)
    pairs = []
    for i in range(size):
        pairs += [(2 * i, 2 * ((i + by) % size)), (2 * i + 1, 2 * ((i - by) % size) + 1)]
    value = jnp.where(lax.axis_index("core") == 0, up, down)
    return lax.ppermute(value, (axis, "core"), pairs)


def ring_step(state, last):
    up, down = state
    if last:
        return shift_apart(up, down, "z")
    return shift(up, "z", 1), shift(down, "z", -1)


def ring_pieces(steps):
    first, *near, last = steps
    return [first[0]] + [u for u, _ in near] + [d for _, d in near[::-1]] + [last]


def on_device(grads):
    width = P_SIZE
    z, yl, yh, x, core = (lax.axis_index(a) for a in AXES)
    k = yh * 4 + x
    mine = lax.dynamic_slice_in_dim(grads, yl * width, width, 1)
    other = lax.dynamic_slice_in_dim(grads, (1 - yl) * width, width, 1)
    swapped = shift(other, "yl", 1)
    rows_a = lax.ppermute(mine, AXES, transpose_perm(1))
    rows_b = lax.ppermute(other, AXES, transpose_perm(0))

    tile = jnp.concatenate([mine, swapped], axis=0)
    curv = lax.dot_general(
        tile, tile, (((0,), (0,)), ((), ())), preferred_element_type=jnp.float32
    )
    packed = pack(curv[:HALF, :HALF], curv[:HALF, HALF:], curv[HALF:, HALF:])
    side = z % 2
    part = PACKED // 2
    keep = lax.dynamic_slice_in_dim(packed, side * part, part, 0)
    give = lax.dynamic_slice_in_dim(packed, (1 - side) * part, part, 0)
    swap_z = lambda v: lax.ppermute(v, "z", [(i, i ^ 1) for i in range(8)])
    sums = after(keep + swap_z(give), (rows_a, rows_b))
    far = shift(after(tile, sums), "yh", 1)
    swap = core == yl
    first = jnp.stack([jnp.where(swap, rows_b, rows_a), jnp.where(swap, rows_a, rows_b)])
    rows = [(first, first)]
    sum_up, sum_down = shift(sums, "z", 2), shift(sums, "z", -2)
    rows.append(ring_step(after(rows[-1], sums), False))
    sum_far = shift_apart(sum_up, sum_down, "z", 2)
    sums = sums + sum_up + sum_down + sum_far
    pair = after(jnp.stack([tile, far]), sum_far)
    up, down = shift(pair, "x", 1), shift(pair, "x", -1)
    back = swap_z(sums)
    rows.append(ring_step(after(rows[-1], back), False))
    total = jnp.where(side == 0, jnp.concatenate([sums, back]), jnp.concatenate([back, sums]))
    inv = call(
        lambda *refs: inverse_kernel(1.0 / (tile.shape[0] * 8), *refs),
        "inverse",
        jax.ShapeDtypeStruct((PACKED, HALF), jnp.float32),
        10**9,
        total,
    )
    inv_far = shift(inv, "yh", 1)
    inv_pair = jnp.stack([inv, inv_far])
    inv_up, inv_down = shift(inv_pair, "x", 1), shift(inv_pair, "x", -1)
    rows.append(ring_step(after(rows[-1], inv_pair), False))
    inv_two = shift_apart(inv_up, inv_down, "x")
    cols_two = shift_apart(*after((up, down), (inv_up, inv_down)), "x")
    rows.append(ring_step(after(rows[-1], (inv_up, inv_down)), True))

    ring = [0, 1, 2, 3, 4, 5, 6, 7]
    half_of = jnp.asarray([[0], [1]], jnp.int32)
    same = (core ^ yl ^ half_of).astype(jnp.int32)
    layer_k = (z - jnp.asarray([ring], jnp.int32) - k - 2 * (2 * same + yl + core)) % 8
    d = (x - layer_k) % 4
    plan = jnp.where(d < 2, 2 * d, 10 - 2 * d) + ((layer_k // 4) ^ yh)

    held = ring_pieces(rows)
    cols = [pair, up, down, cols_two]
    half = mine.shape[0]
    parts = split([inv_pair, inv_up, inv_down])
    precond = precondition(plan, [parts], held[:7])
    precond = precondition(plan, [parts, split([inv_two])], held, precond)
    theirs, other = partial_gram(precond, cols, half)
    from_core = shift(theirs, "core", 1)
    total_other = (other + from_core).astype(jnp.bfloat16)
    got = shift(total_other, "yl", 1)
    theirs, own = partial_gram(after(precond, theirs), cols, 0)
    own_core = shift(theirs, "core", 1)
    scale = 1.0 / jnp.float32(32 * width)
    return (own + own_core + got.astype(jnp.float32)) * scale


def solution(mesh):
    fine = Mesh(mesh.devices.reshape(SIZES), AXES)
    return jax.shard_map(
        on_device,
        mesh=fine,
        in_specs=(P(("z", "yl"), ("yh", "x", "core")),),
        out_specs=P(("yh", "x", "core"), ("z", "yl")),
        check_vma=False,
    )
```

```python
import jax
import jax.numpy as jnp
from jax import lax
from jax.experimental import pallas as pl
from jax.experimental.pallas import tpu as pltpu
from jax.sharding import Mesh, PartitionSpec as P

P_SIZE = 256
HALF = 128
QUARTER = 64
PACKED = 320
PANEL = 8
RIDGE = 0.1
AXES = ("z", "yl", "yh", "x", "core")
SIZES = (8, 2, 2, 4, 2)
HIGHEST = lax.Precision.HIGHEST


def dot32(a, b):
    return jnp.dot(a, b, precision=HIGHEST, preferred_element_type=jnp.float32)


def invert_block(d):
    n = d.shape[0]
    lane = lax.broadcasted_iota(jnp.int32, (1, n), 1)
    sub = lax.broadcasted_iota(jnp.int32, (PANEL, n), 0)
    for k in range(0, n, PANEL):
        cols = [jnp.broadcast_to(d[:, k + i : k + i + 1], (n, n)) for i in range(PANEL)]
        piv = [c[k : k + PANEL, :] for c in cols]
        for j in range(PANEL):
            rp = 1.0 / piv[j][j : j + 1, :]
            pj = piv[j]
            for i in range(PANEL):
                if i == j:
                    piv[i] = jnp.where(sub == j, rp, -pj * rp)
                else:
                    w = piv[i][j : j + 1, :] * rp
                    piv[i] = jnp.where(sub == j, w, piv[i] - pj * w)
        rows = d[k : k + PANEL, :]
        new = piv[0] * rows[0:1, :]
        for i in range(1, PANEL):
            new = new + piv[i] * rows[i : i + 1, :]
        for i in range(PANEL):
            new = jnp.where(lane == k + i, piv[i], new)
        d = jnp.where((lane >= k) & (lane < k + PANEL), 0.0, d)
        for i in range(PANEL):
            d = d - cols[i] * new[i : i + 1, :]
        parts = [x for x in (d[:k], new, d[k + PANEL :]) if x.shape[0]]
        d = jnp.concatenate(parts, axis=0)
    return d


def pack(a11, a12, a22):
    q = QUARTER
    corners = jnp.concatenate([a11[q:, q:], a22[q:, q:]], axis=1)
    return jnp.concatenate([a11[:q], a12, a22[:q], corners], axis=0)


def unpack(packed):
    q = QUARTER
    corners = packed[4 * q :]

    def whole(top, corner):
        low = jnp.concatenate([top[:, q:].T, corner], axis=1)
        return jnp.concatenate([top, low], axis=0)

    a11 = whole(packed[:q], corners[:, :q])
    a22 = whole(packed[3 * q : 4 * q], corners[:, q:])
    return a11, packed[q : 3 * q], a22


def ridge():
    r0 = lax.broadcasted_iota(jnp.int32, (HALF, HALF), 0)
    r1 = lax.broadcasted_iota(jnp.int32, (HALF, HALF), 1)
    return jnp.where(r0 == r1, jnp.float32(RIDGE), 0.0)


def first_kernel(scale, total, inv11):
    a11, _, _ = unpack(total[...] * scale)
    inv11[...] = invert_block(a11 + ridge())


def second_kernel(scale, total, inv11, out):
    _, a12, a22 = unpack(total[...] * scale)
    inv = inv11[...]
    y = dot32(inv, a12)
    z = invert_block(a22 + ridge() - dot32(a12.T, y))
    w = -dot32(y, z)
    out[...] = pack(inv - dot32(w, y.T), w, z)


VMEM = pl.BlockSpec(memory_space=pltpu.VMEM)
SMEM = pl.BlockSpec(memory_space=pltpu.SMEM)


def call(kernel, name, shape, flops, *operands, specs=None, aliases=None):
    return pl.pallas_call(
        kernel,
        in_specs=specs or [VMEM] * len(operands),
        out_specs=jax.tree.map(lambda _: VMEM, shape),
        out_shape=shape,
        input_output_aliases=aliases or {},
        compiler_params=pltpu.CompilerParams(vmem_limit_bytes=16 * 1024 * 1024),
        cost_estimate=pl.CostEstimate(
            flops=flops, bytes_accessed=4 * 10**6, transcendentals=0
        ),
        name=name,
    )(*operands)


def split_kernel(*refs):
    out = refs[-1]
    matrices = [r[j] for r in refs[:-1] for j in range(r.shape[0])]
    for t, packed in enumerate(matrices):
        top, off, low = unpack(packed)
        full = jnp.concatenate(
            [jnp.concatenate([top, off], axis=1), jnp.concatenate([off.T, low], axis=1)],
            axis=0,
        )
        for i in range(3):
            part = full.astype(jnp.bfloat16)
            full = full - part.astype(jnp.float32)
            out[t, i * P_SIZE : (i + 1) * P_SIZE] = part


def split(inv):
    layers = sum(i.shape[0] for i in inv)
    shape = jax.ShapeDtypeStruct((layers, 3 * P_SIZE, P_SIZE), jnp.bfloat16)
    return call(split_kernel, "split", shape, 10**6, *inv)


def precond_kernel(late, plan, *refs):
    *parts, out = refs[: 2 if late else 1] + (refs[-1],)
    tiles = refs[len(parts) : len(parts) + 8 if late else len(parts) + 7]
    near = parts[0].shape[0]
    slot = 0
    for n, r in enumerate(tiles):
        for j in range(r.shape[0]):
            step = (0, 1, 2, 3, 5, 6, 7, 4)[n]
            layer = plan[j, step]

            def put(part):
                x = r[j]
                total = jnp.dot(
                    jnp.concatenate([x, x, x], axis=1), part, preferred_element_type=jnp.float32
                )
                across = pl.ds(pl.multiple_of(plan[2 + j, step] * P_SIZE, P_SIZE), P_SIZE)
                count = x.shape[0]
                out[j * count : (j + 1) * count, across] = total.astype(jnp.bfloat16)

            if not late or step == 4:

                @pl.when(layer < near)
                def _():
                    put(parts[0][layer])

            if late:

                @pl.when(layer >= near)
                def _():
                    put(parts[1][layer - near])


def precondition(plan, parts, rows, into=None):
    late = into is not None
    count = rows[0].shape[1]
    shape = jax.ShapeDtypeStruct((2 * count, 8 * P_SIZE), jnp.bfloat16)
    operands = [plan, *parts, *rows] + ([into] if late else [])
    return call(
        lambda *refs: precond_kernel(late, *refs),
        "precondition",
        shape,
        6 * 10**9,
        *operands,
        specs=[SMEM] + [VMEM] * (len(operands) - 1),
        aliases={len(operands) - 1: 0} if late else None,
    )


def gram_kernel(start, precond, *refs):
    theirs, mine = refs[-2:]
    half = mine.shape[1]
    cols = [r[j, start : start + half] for r in refs[:-2] for j in range(r.shape[0])]
    total = lax.dot_general(
        precond[...],
        jnp.concatenate(cols, axis=1),
        (((1,), (1,)), ((), ())),
        preferred_element_type=jnp.float32,
    )
    theirs[...] = total[: theirs.shape[0]]
    mine[...] = total[theirs.shape[0] :]


def partial_gram(precond, cols, start):
    half = cols[0].shape[1] // 2
    shape = [jax.ShapeDtypeStruct((precond.shape[0] // 2, half), jnp.float32)] * 2
    return call(
        lambda *refs: gram_kernel(start, *refs), "gram", shape, 2 * 10**9, precond, *cols
    )


def shift(value, axis, by):
    size = lax.axis_size(axis)
    return lax.ppermute(value, axis, [(i, (i + by) % size) for i in range(size)])


def flat_index(z, yl, yh, x, core):
    return (((z * 2 + yl) * 2 + yh) * 4 + x) * 2 + core


def after(values, token):
    return lax.optimization_barrier((values, token))[0]


def transpose_perm(same):
    pairs = []
    for z in range(8):
        for y in range(2):
            for k in range(8):
                for b in range(2):
                    src = flat_index(z, y, k // 4, k % 4, b)
                    p = y if same else 1 - y
                    to = (z + k + 2 * (2 * same + p + b)) % 8
                    pairs.append((src, flat_index(to, p, z // 4, z % 4, b)))
    return pairs


def shift_apart(up, down, axis, by=1):
    size = lax.axis_size(axis)
    pairs = []
    for i in range(size):
        pairs += [(2 * i, 2 * ((i + by) % size)), (2 * i + 1, 2 * ((i - by) % size) + 1)]
    value = jnp.where(lax.axis_index("core") == 0, up, down)
    return lax.ppermute(value, (axis, "core"), pairs)


def ring_step(state, last):
    up, down = state
    if last:
        return shift_apart(up, down, "z")
    return shift(up, "z", 1), shift(down, "z", -1)


def ring_pieces(steps):
    first, *near, last = steps
    return [first[0]] + [u for u, _ in near] + [d for _, d in near[::-1]] + [last]


def on_device(grads):
    width = P_SIZE
    z, yl, yh, x, core = (lax.axis_index(a) for a in AXES)
    k = yh * 4 + x
    mine = lax.dynamic_slice_in_dim(grads, yl * width, width, 1)
    other = lax.dynamic_slice_in_dim(grads, (1 - yl) * width, width, 1)
    swapped = shift(other, "yl", 1)
    rows_a = lax.ppermute(mine, AXES, transpose_perm(1))
    rows_b = lax.ppermute(other, AXES, transpose_perm(0))

    tile = jnp.concatenate([mine, swapped], axis=0)
    curv = lax.dot_general(
        tile, tile, (((0,), (0,)), ((), ())), preferred_element_type=jnp.float32
    )
    packed = pack(curv[:HALF, :HALF], curv[:HALF, HALF:], curv[HALF:, HALF:])
    side = z % 2
    part = PACKED // 2
    keep = lax.dynamic_slice_in_dim(packed, side * part, part, 0)
    give = lax.dynamic_slice_in_dim(packed, (1 - side) * part, part, 0)
    swap_z = lambda v: lax.ppermute(v, "z", [(i, i ^ 1) for i in range(8)])
    sums = after(keep + swap_z(give), (rows_a, rows_b))
    far = shift(after(tile, sums), "yh", 1)
    swap = core == yl
    first = jnp.stack([jnp.where(swap, rows_b, rows_a), jnp.where(swap, rows_a, rows_b)])
    rows = [(first, first)]
    sum_up, sum_down = shift(sums, "z", 2), shift(sums, "z", -2)
    rows.append(ring_step(after(rows[-1], sums), False))
    sum_far = shift_apart(sum_up, sum_down, "z", 2)
    sums = sums + sum_up + sum_down + sum_far
    cols = [after(jnp.stack([tile, far]), sum_up)]
    cols.append(shift_apart(cols[0], cols[0], "x"))
    back = swap_z(after(sums, far))
    rows.append(ring_step(after(rows[-1], back), False))
    total = jnp.where(side == 0, jnp.concatenate([sums, back]), jnp.concatenate([back, sums]))
    over = 1.0 / (tile.shape[0] * 8)
    inv11 = call(
        lambda *refs: first_kernel(over, *refs),
        "inverse_first",
        jax.ShapeDtypeStruct((HALF, HALF), jnp.float32),
        6 * 10**9,
        total,
    )
    late = after(cols[1], inv11)
    cols.append(shift_apart(late, late, "x"))
    inv = call(
        lambda *refs: second_kernel(over, *refs),
        "inverse_second",
        jax.ShapeDtypeStruct((PACKED, HALF), jnp.float32),
        6 * 10**9,
        *after((total, inv11), cols[1]),
    )
    inv_far = shift(inv, "yh", 1)
    inv_pair = after(jnp.stack([inv, inv_far]), cols[2])
    inv_up, inv_down = shift(inv_pair, "x", 1), shift(inv_pair, "x", -1)
    rows.append(ring_step(after(rows[-1], inv_pair), False))
    inv_two = shift_apart(inv_up, inv_down, "x")
    late = after(cols[2], inv_two)
    cols.append(shift_apart(late, late, "x"))
    rows.append(ring_step(rows[-1], True))

    ring = [0, 1, 2, 3, 4, 5, 6, 7]
    half_of = jnp.asarray([[0], [1]], jnp.int32)
    same = (core ^ yl ^ half_of).astype(jnp.int32)
    layer_k = (z - jnp.asarray([ring], jnp.int32) - k - 2 * (2 * same + yl + core)) % 8
    d = (x - layer_k) % 4
    by_inv = jnp.where(d < 2, 2 * d, 10 - 2 * d) + ((layer_k // 4) ^ yh)
    by_cols = 2 * jnp.where(core == 0, d, (4 - d) % 4) + ((layer_k // 4) ^ yh)
    plan = jnp.concatenate([by_inv, by_cols])

    held = ring_pieces(rows)
    half = mine.shape[0]
    parts = split([inv_pair, inv_up, inv_down])
    precond = precondition(plan, [parts], held[:7])
    precond = precondition(plan, [parts, split([inv_two])], held, precond)
    theirs, other = partial_gram(precond, cols, half)
    from_core = shift(theirs, "core", 1)
    total_other = (other + from_core).astype(jnp.bfloat16)
    got = shift(total_other, "yl", 1)
    theirs, own = partial_gram(after(precond, theirs), cols, 0)
    own_core = shift(theirs, "core", 1)
    scale = 1.0 / jnp.float32(32 * width)
    return (own + own_core + got.astype(jnp.float32)) * scale


def solution(mesh):
    fine = Mesh(mesh.devices.reshape(SIZES), AXES)
    return jax.shard_map(
        on_device,
        mesh=fine,
        in_specs=(P(("z", "yl"), ("yh", "x", "core")),),
        out_specs=P(("yh", "x", "core"), ("z", "yl")),
        check_vma=False,
    )
```
